32 devices in a mesh: axial: 4 (over y, core), azim: 8 (over z, x).
Axes of the slice: x: 2, y: 2, z: 4, core: 2. Of those that a mesh axis runs over, the one named last changes fastest.
Arguments:
- state: float32 [5, 64, 131072], P(None, 'axial', 'azim'), may hold values from -6 to 6
- profile: float32 [64, 131072], P(None, ('axial', 'azim')), may hold values from -6 to 6
- samp_cell: int32 [32, 32, 128], P(('axial', 'azim')), may hold values from 0 to 262143
- own_live: int32 [32], replicated, may hold values from 1 to 4096, 65536 in all
Outputs:
- new_profile: float32 [64, 131072], P(None, ('axial', 'azim'))
- wall_stress: float32 [2, 131072], P(None, ('axial', 'azim'))
The draws below stay inside these ranges and needn't reach their ends.
Inputs may be any that keep to these rules, and one draw needn't show every extreme that they name: own_live sums to 32 * 4096 // 2 over all owners.
All inputs are finite; a program needn't handle non-finite values.
Results may differ from the reference program's by a relative error of at most 0.0003.
Values sent between devices are 32-bit elements; how exact they have to be, the bound alone decides.
A program may use at most 320 MiB of HBM per device.

```python
import math
import jax
import jax.numpy as jnp
import numpy as np
from jax import lax

Q = 5
NW = 64
ITERS = 3
CX = 16
CT = 16384
OWN = 4096
SCAP = 128
NX = 64
NT = 131072
N_AXIAL = 4
N_AZIM = 8
DEVICES = 32


def set_ends(entries, own_key, least, top_value):
    extent = entries.shape
    index_at = [jax.random.randint(jax.random.fold_in(own_key, axis), (), 0, extent[axis]) for axis in range(len(extent))]
    entries = entries.at[tuple(index_at)].set(least)
    longest = extent.index(max(extent))
    index_at[longest] = (index_at[longest] + 1) % extent[longest]
    return entries.at[tuple(index_at)].set(top_value)


def block_scale(own_key, extent, cuts, low, high):
    def one(axis_at, shards_of):
        heights = jax.random.uniform(jax.random.fold_in(jax.random.fold_in(own_key, 6), axis_at), (shards_of,), jnp.float32, low / len(cuts), high / len(cuts))
        return jnp.repeat(jnp.exp(heights), extent[axis_at] // shards_of).reshape((-1,) + (1,) * (len(extent) - axis_at - 1))

    level = one(*cuts[0])
    for cut in cuts[1:]:
        level = level * one(*cut)
    return level


def split_up(number_of, total, most, skew):
    weights = [(1 << 20) // math.isqrt(rank ** skew) + 1 for rank in range(2, number_of + 1)]
    rest, counts = total - most - (number_of - 1), [1] * (number_of - 1)
    while rest > 0:
        candidates = [i for i in range(number_of - 1) if counts[i] < most]
        pool, remaining = sum([weights[i] for i in candidates]), rest
        for i in candidates:
            extra = min(most - counts[i], max(1, remaining * weights[i] // pool), rest)
            counts[i] = counts[i] + extra
            rest = rest - extra
    return np.array([most] + counts)


def uneven(key, amount, total, bound, skew):
    if amount == 2:
        one = jax.random.randint(key, (), max(1, total - bound), min(bound, total - 1) + 1)
        return jnp.stack([one, total - one])
    tallies = jnp.asarray(split_up(amount, total, bound, skew), jnp.int32)
    twos = (amount - 1) // 2
    giver, receiver = tallies[1:1 + 2 * twos:2], tallies[2:2 + 2 * twos:2]
    slack = jnp.minimum(giver - 1, bound - receiver)
    moved = jax.random.randint(jax.random.fold_in(key, 1), (twos,), 0, 1 << 20) % (slack + 1)
    tallies = tallies.at[1:1 + 2 * twos:2].set(giver - moved).at[2:2 + 2 * twos:2].set(receiver + moved)
    return tallies[jax.random.permutation(jax.random.fold_in(key, 2), amount)]


def normal_values(own_key, shape, width, limit, cuts=(), kind=jnp.bfloat16):
    entries = width * jax.random.normal(own_key, shape, jnp.float32)
    if cuts:
        entries = entries * block_scale(own_key, shape, cuts, -0.22, 0.18)
    return jnp.clip(entries, -limit, limit).astype(kind)


def setup_inputs(seed: int = 0) -> dict:
    streams_of = jax.random.split(jax.random.key(seed), 5)
    return {
        "state": normal_values(streams_of[0], (Q, NX, NT), 1.0, 6.0, ((1, 4), (2, 8)), jnp.float32),
        "profile": normal_values(streams_of[1], (NW, DEVICES * OWN), 1.0, 6.0, ((1, 32),), jnp.float32),
        "samp_cell": set_ends(jax.random.randint(streams_of[2], (DEVICES, DEVICES, SCAP), 0, CX * CT), jax.random.fold_in(streams_of[2], 1), 0, (CX * CT) - 1).astype(jnp.int32),
        "own_live": uneven(streams_of[3], DEVICES, DEVICES * OWN // 2, OWN, 2).astype(jnp.int32),
    }


def thomas(lower_rows, diag_rows, upper_rows, rhs_rows):
    count = len(rhs_rows)
    zeros = jnp.zeros_like(rhs_rows[0])
    c_prev = zeros
    d_prev = zeros
    c_list = []
    d_list = []
    for row in range(count):
        denom = diag_rows[row] - lower_rows[row] * c_prev
        c_new = upper_rows[row] / denom
        d_new = (rhs_rows[row] - lower_rows[row] * d_prev) / denom
        c_list.append(c_new)
        d_list.append(d_new)
        c_prev = c_new
        d_prev = d_new
    after = zeros
    values = [zeros] * count
    for row in range(count - 1, -1, -1):
        after = d_list[row] - c_list[row] * after
        values[row] = after
    return jnp.stack(values, axis=0)

def wall_solve(profile, match):
    points = profile.shape[0]
    step = 1.0 / (points - 1)
    density = jnp.exp(0.3 * match[0])
    vel_ax = match[1]
    vel_az = match[2]
    source = 0.5 * match[3]
    visc = 0.01 * jnp.exp(0.5 * match[4])
    speed = jnp.sqrt(vel_ax * vel_ax + vel_az * vel_az + 0.25)
    mixing = 0.41 * (jnp.arange(points - 1, dtype=jnp.float32) + 0.5) * step
    mix_sq = (mixing * mixing)[:, None]
    zero_row = jnp.zeros_like(profile[0])
    one_row = jnp.ones_like(profile[0])
    velocity = profile
    for sweep in range(ITERS):
        grad = (velocity[1:] - velocity[:-1]) / step
        root = jnp.sqrt(grad * grad + 1.0)
        flux = (visc + mix_sq * root) * grad
        slope = visc + mix_sq * (root + grad * grad / root)
        inner = -(step * (flux[1:] - flux[:-1]) - source * step * step)
        lower_rows = [zero_row] + [slope[i - 1] for i in range(1, points - 1)] + [zero_row]
        upper_rows = [zero_row] + [slope[i] for i in range(1, points - 1)] + [zero_row]
        diag_rows = [one_row] + [-(slope[i] + slope[i - 1]) for i in range(1, points - 1)] + [one_row]
        rhs_rows = [-velocity[0]] + [inner[i - 1] for i in range(1, points - 1)] + [speed - velocity[-1]]
        velocity = velocity + thomas(lower_rows, diag_rows, upper_rows, rhs_rows)
    shear = density * visc * (velocity[1] - velocity[0]) / step
    stress = jnp.stack([shear * vel_ax / speed, shear * vel_az / speed], axis=0)
    return (velocity, stress)

def reference(state, profile, samp_cell, own_live):
    devices = N_AXIAL * N_AZIM
    filtered = 0.25 * jnp.roll(state, 1, axis=1) + 0.5 * state + 0.25 * jnp.roll(state, -1, axis=1)
    source_dev = jnp.arange(devices, dtype=jnp.int32)[:, None, None]
    row_x = source_dev // N_AZIM * CX + samp_cell // CT
    row_t = source_dev % N_AZIM * CT + samp_cell % CT
    picked = filtered[:, row_x, row_t]
    match = picked.transpose(0, 2, 1, 3).reshape(Q, devices, OWN).transpose(1, 0, 2)
    stored = profile.reshape(NW, devices, OWN).transpose(1, 0, 2)
    solved, stress = lax.map(lambda pair: wall_solve(pair[0], pair[1]), (stored, match))
    burning = jnp.arange(OWN, dtype=jnp.int32)[None, :] < own_live[:, None]
    solved = jnp.where(burning[:, None, :], solved, stored)
    stress = jnp.where(burning[:, None, :], stress, jnp.float32(0.0))
    new_profile = solved.transpose(1, 0, 2).reshape(NW, devices * OWN)
    wall_stress = stress.transpose(1, 0, 2).reshape(2, devices * OWN)
    return (new_profile, wall_stress)
```

```python
import functools

import jax
import jax.numpy as jnp
from jax import lax
from jax.experimental import pallas as pl
from jax.experimental.pallas import tpu as pltpu
from jax.sharding import PartitionSpec as P

ITERS = 3
AXES = ("axial", "azim")
SUB = 8
LANE = 128


def smooth_planes(raw, filt, stride, tiles_x, sections, sems, state):
    comps = state.shape[0]
    sub = lax.broadcasted_iota(jnp.int32, (SUB, LANE), 0)
    for q in range(comps):
        pltpu.make_async_copy(state.at[q], raw.at[q], sems.at[q]).wait()

        def section(tb, carry):
            tiles = [raw[q, pl.ds((xt * sections + tb) * SUB, SUB), :] for xt in range(tiles_x)]
            ups = [pltpu.roll(tile, 1, 0) for tile in tiles]
            downs = [pltpu.roll(tile, SUB - 1, 0) for tile in tiles]
            for xt in range(tiles_x):
                below = ups[xt - 1] if xt > 0 else 0.0
                above = downs[xt + 1] if xt + 1 < tiles_x else 0.0
                low = jnp.where(sub == 0, below, ups[xt])
                high = jnp.where(sub == SUB - 1, above, downs[xt])
                at = q * stride + (xt * sections + tb) * SUB
                filt[pl.ds(pl.multiple_of(at, SUB), SUB), :] = 0.25 * (low + high) + 0.5 * tiles[xt]
            return carry

        lax.fori_loop(0, sections, section, 0, unroll=8)


def add_halo(filt, halo, start, stride, sections):
    comps = halo.shape[0]
    for q in range(comps):
        for g in range(sections // SUB):
            rows = pl.ds(q * stride + start + g * SUB * SUB, SUB, stride=SUB)
            filt[rows, :] = filt[rows, :] + 0.25 * halo[q, pl.ds(g * SUB, SUB), :]


def gather_kernel(tiles_x, sections, stride, rows, lanes, state, low, high, out, raw, filt, sems):
    comps = state.shape[0]
    groups = out.shape[0]
    for q in range(comps):
        pltpu.make_async_copy(state.at[q], raw.at[q], sems.at[q]).start()
    smooth_planes(raw, filt, stride, tiles_x, sections, sems, state)
    add_halo(filt, low, 0, stride, sections)
    add_halo(filt, high, (tiles_x - 1) * sections * SUB + SUB - 1, stride, sections)
    lane = lax.broadcasted_iota(jnp.int32, (SUB, LANE), 1)

    def group(e, carry):
        wanted = jnp.broadcast_to(lanes[pl.ds(e, 1), :], (SUB, LANE))
        found = jnp.zeros((SUB, LANE), jnp.float32)
        for k in range(LANE):
            cell = filt[pl.ds(rows[e, k], SUB, stride=stride), :]
            cell = jnp.take_along_axis(cell, wanted, axis=1)
            found = jnp.where(lane == k, cell, found)
        out[e] = found
        return carry

    lax.fori_loop(0, groups, group, 0)


def solve_kernel(points, width, live, profile, match, new_profile, wall_stress):
    step = 1.0 / (points - 1)
    inv_step = float(points - 1)
    tiles = points // SUB
    sub = lax.broadcasted_iota(jnp.int32, (SUB, LANE), 0)
    lane = lax.broadcasted_iota(jnp.int32, (1, LANE), 1)
    index = [(sub + t * SUB).astype(jnp.float32) for t in range(tiles)]
    mixing = [0.41 * (i + 0.5) * step for i in index]
    mix_sq = [m * m for m in mixing]
    first = pl.program_id(0) * width

    def spread(row):
        return jnp.broadcast_to(row, (SUB, LANE))

    for cb in range(width // LANE):
        cols = pl.ds(cb * LANE, LANE)
        m = [spread(match[cb, q : q + 1, :]) for q in range(5)]
        visc = 0.01 * jnp.exp(0.5 * m[4])
        sigma = (0.5 * step) * m[3]
        speed = jnp.sqrt(m[1] * m[1] + m[2] * m[2] + 0.25)
        old = [profile[pl.ds(t * SUB, SUB), cols] for t in range(tiles)]
        turned = [pltpu.roll(u, SUB - 1, 0) for u in old]
        grad = []
        for t in range(tiles):
            after = turned[t + 1] if t + 1 < tiles else old[t]
            grad.append((jnp.where(sub == SUB - 1, after, turned[t]) - old[t]) * inv_step)
        for sweep in range(ITERS):
            weight_sum = jnp.zeros((SUB, LANE), jnp.float32)
            known_sum = jnp.zeros((SUB, LANE), jnp.float32)
            weights = []
            knowns = []
            for t in range(tiles):
                square = grad[t] * grad[t]
                over = square + 1.0
                inv_root = lax.rsqrt(over)
                viscous = visc + mix_sq[t] * (over * inv_root)
                excess = mix_sq[t] * (square * inv_root)
                weight = 1.0 / (viscous + excess)
                if t == tiles - 1:
                    weight = jnp.where(sub == SUB - 1, 0.0, weight)
                known = (excess * grad[t] + sigma * index[t]) * weight
                weight_sum = weight_sum + weight
                known_sum = known_sum + known
                weights.append(weight)
                knowns.append(known)
            weight_all = spread(jnp.sum(weight_sum, axis=0, keepdims=True))
            known_all = spread(jnp.sum(known_sum, axis=0, keepdims=True))
            flux = (inv_step * speed - known_all) / weight_all
            grad = [knowns[t] + flux * weights[t] for t in range(tiles)]
        burning = lane + (first + cb * LANE) < live[0]
        burn = spread(burning.astype(jnp.int32)) > 0
        carry = jnp.zeros((SUB, LANE), jnp.float32)
        for t in range(tiles):
            total = grad[t]
            for hop in (1, 2, 4):
                total = total + jnp.where(sub >= hop, pltpu.roll(total, hop, 0), 0.0)
            before = jnp.where(sub >= 1, pltpu.roll(total, 1, 0), 0.0)
            new_profile[pl.ds(t * SUB, SUB), cols] = jnp.where(
                burn, (before + carry) * step, old[t]
            )
            carry = carry + spread(total[SUB - 1 : SUB, :])
        shear = jnp.exp(0.3 * m[0]) * visc * spread(grad[0][0:1, :])
        for row, part in enumerate((m[1], m[2])):
            wall_stress[row : row + 1, cols] = jnp.where(burn, shear * part / speed, 0.0)[0:1, :]


def solve(profile, match, live):
    points, owned = profile.shape
    width = min(1024, owned)
    return pl.pallas_call(
        functools.partial(solve_kernel, points, width),
        grid=(owned // width,),
        out_shape=(
            jax.ShapeDtypeStruct((points, owned), jnp.float32),
            jax.ShapeDtypeStruct((2, owned), jnp.float32),
        ),
        in_specs=[
            pl.BlockSpec(memory_space=pltpu.SMEM),
            pl.BlockSpec((points, width), lambda i: (0, i)),
            pl.BlockSpec((width // LANE, SUB, LANE), lambda i: (i, 0, 0)),
        ],
        out_specs=(
            pl.BlockSpec((points, width), lambda i: (0, i)),
            pl.BlockSpec((2, width), lambda i: (0, i)),
        ),
        compiler_params=pltpu.CompilerParams(vmem_limit_bytes=32 << 20),
        name="wall_solve",
    )(live, profile, match)


def body(state, profile, samp_cell, own_live):
    comps, slab, section = state.shape
    owned = profile.shape[1]
    devices = lax.axis_size(AXES)
    slots = samp_cell.shape[2]
    here = lax.axis_index(AXES)
    groups = owned // LANE
    tiles_x = slab // SUB
    sections = section // LANE
    plane = slab * sections
    stride = plane + SUB
    cells = samp_cell.reshape(groups, LANE)
    at_x = cells // section
    at_t = cells % section
    rows = ((at_x // SUB) * sections + at_t // LANE) * SUB + at_x % SUB
    lanes = at_t % LANE
    count = lax.axis_size("axial")
    forward = [(i, (i + 1) % count) for i in range(count)]
    backward = [((i + 1) % count, i) for i in range(count)]
    low = lax.ppermute(state[:, slab - 1, :], "axial", forward).reshape(comps, sections, LANE)
    high = lax.ppermute(state[:, 0, :], "axial", backward).reshape(comps, sections, LANE)
    view = state.reshape(comps, tiles_x, SUB, sections, LANE)
    view = view.transpose(0, 1, 3, 2, 4).reshape(comps, plane, LANE)
    sampled = pl.pallas_call(
        functools.partial(gather_kernel, tiles_x, sections, stride),
        out_shape=jax.ShapeDtypeStruct((groups, SUB, LANE), jnp.float32),
        in_specs=[
            pl.BlockSpec(memory_space=pltpu.SMEM),
            pl.BlockSpec(memory_space=pltpu.VMEM),
            pl.BlockSpec(memory_space=pl.ANY),
            pl.BlockSpec(memory_space=pltpu.VMEM),
            pl.BlockSpec(memory_space=pltpu.VMEM),
        ],
        out_specs=pl.BlockSpec(memory_space=pltpu.VMEM),
        scratch_shapes=[
            pltpu.VMEM((comps, plane, LANE), jnp.float32),
            pltpu.VMEM((SUB * stride, LANE), jnp.float32),
            pltpu.SemaphoreType.DMA((comps,)),
        ],
        compiler_params=pltpu.CompilerParams(vmem_limit_bytes=40 << 20),
        name="sample_cells",
    )(rows, lanes, view, low, high)
    if slots == LANE:
        match = lax.all_to_all(sampled, AXES, split_axis=0, concat_axis=0, tiled=True)
    else:
        outgoing = sampled.transpose(1, 0, 2).reshape(SUB, devices, slots)
        arrived = lax.all_to_all(outgoing, AXES, split_axis=1, concat_axis=1, tiled=True)
        match = arrived.reshape(SUB, groups, LANE).transpose(1, 0, 2)
    live = lax.dynamic_slice(own_live, (here,), (1,))
    return solve(profile, match, live)


def solution(mesh):
    return jax.shard_map(
        body,
        mesh=mesh,
        in_specs=(
            P(None, "axial", "azim"),
            P(None, AXES),
            P(AXES, None, None),
            P(),
        ),
        out_specs=(P(None, AXES), P(None, AXES)),
        check_vma=False,
    )
```

```python
import functools

import jax
import jax.numpy as jnp
from jax import lax
from jax.experimental import pallas as pl
from jax.experimental.pallas import tpu as pltpu
from jax.sharding import PartitionSpec as P

ITERS = 3
AXES = ("axial", "azim")
SUB = 8
LANE = 128


def smooth_planes(raw, filt, stride, tiles_x, sections, sems, state):
    comps = state.shape[0]
    sub = lax.broadcasted_iota(jnp.int32, (SUB, LANE), 0)
    for q in range(comps):
        pltpu.make_async_copy(state.at[q], raw.at[q], sems.at[q]).wait()

        def section(tb, carry):
            tiles = [raw[q, xt, tb] for xt in range(tiles_x)]
            ups = [pltpu.roll(tile, 1, 0) for tile in tiles]
            downs = [pltpu.roll(tile, SUB - 1, 0) for tile in tiles]
            for xt in range(tiles_x):
                below = ups[xt - 1] if xt > 0 else 0.0
                above = downs[xt + 1] if xt + 1 < tiles_x else 0.0
                low = jnp.where(sub == 0, below, ups[xt])
                high = jnp.where(sub == SUB - 1, above, downs[xt])
                at = q * stride + (xt * sections + tb) * SUB
                filt[pl.ds(pl.multiple_of(at, SUB), SUB), :] = 0.25 * (low + high) + 0.5 * tiles[xt]
            return carry

        lax.fori_loop(0, sections, section, 0, unroll=8)


def add_halo(filt, halo, start, sections):
    for g in range(sections // SUB):
        rows = pl.ds(start + g * SUB * SUB, SUB, stride=SUB)
        filt[rows, :] = filt[rows, :] + 0.25 * halo[pl.ds(g * SUB, SUB), :]


def sample_kernel(
    names,
    sizes,
    cells,
    state,
    out,
    raw,
    filt,
    halo,
    stage,
    rows_v,
    rows,
    sems,
    halo_send,
    halo_recv,
    row_sem,
    send_sem,
    recv_sem,
):
    tiles_x, sections, stride = sizes
    comps = state.shape[0]
    groups = stage.shape[0]
    devices = out.shape[0]
    share = devices // groups
    axial, azim = names
    a, z = lax.axis_index(axial), lax.axis_index(azim)
    count, width = lax.axis_size(axial), lax.axis_size(azim)
    me = a * width + z

    def place(d):
        return (d // width, d % width)

    for q in range(comps):
        pltpu.make_async_copy(state.at[q], raw.at[q], sems.at[q]).start()

    barrier = pltpu.get_barrier_semaphore()

    def greet(j, carry):
        pl.semaphore_signal(
            barrier, inc=1, device_id=place((me + j) % devices), device_id_type=pl.DeviceIdType.MESH
        )
        return carry

    lax.fori_loop(1, devices, greet, 0)

    cell = cells[...]
    section = sections * LANE
    at_x = cell // section
    at_t = cell % section
    rows_v[...] = ((at_x // SUB) * sections + at_t // LANE) * SUB + at_x % SUB
    row_copy = pltpu.make_async_copy(rows_v, rows, row_sem)
    row_copy.start()
    pl.semaphore_wait(barrier, devices - 1)

    halos = []
    for q in range(comps):
        for side in range(2):
            if side == 0:
                edge = state.at[q, tiles_x - 1, :, SUB - 1, :]
                target = (a + 1) % count
            else:
                edge = state.at[q, 0, :, 0, :]
                target = (a + count - 1) % count
            copy = pltpu.make_async_remote_copy(
                src_ref=edge,
                dst_ref=halo.at[side, q],
                send_sem=halo_send.at[side, q],
                recv_sem=halo_recv.at[side, q],
                device_id=(target, z),
                device_id_type=pl.DeviceIdType.MESH,
            )
            copy.start()
            halos.append(copy)

    filt[pl.ds(comps * stride, (SUB - comps) * stride), :] = jnp.zeros(
        ((SUB - comps) * stride, LANE), jnp.float32
    )
    smooth_planes(raw, filt, stride, tiles_x, sections, sems, state)
    last = (tiles_x - 1) * sections * SUB + SUB - 1
    for q in range(comps):
        for side in range(2):
            halos[2 * q + side].wait()
            add_halo(filt, halo.at[side, q], q * stride + (0 if side == 0 else last), sections)
    row_copy.wait()
    lane = lax.broadcasted_iota(jnp.int32, (SUB, LANE), 1)

    def group(j, carry):
        g = (me // share + 1 + j) % groups
        wanted = jnp.broadcast_to(cells[pl.ds(g, 1), :] % LANE, (SUB, LANE))
        found = jnp.zeros((SUB, LANE), jnp.float32)
        for k in range(LANE):
            piece = filt[pl.ds(rows[g, k], SUB, stride=stride), :]
            piece = jnp.take_along_axis(piece, wanted, axis=1)
            found = jnp.where(lane == k, piece, found)
        stage[g] = found
        for r in range(share):
            owner = g * share + r

            @pl.when(owner != me)
            def _():
                pltpu.make_async_remote_copy(
                    src_ref=stage.at[g],
                    dst_ref=out.at[me],
                    send_sem=send_sem,
                    recv_sem=recv_sem,
                    device_id=place(owner),
                    device_id_type=pl.DeviceIdType.MESH,
                ).start()

            @pl.when(owner == me)
            def _():
                out[me] = found

        return carry

    lax.fori_loop(0, groups, group, 0)
    every = out.at[pl.ds(0, devices - 1)]
    pltpu.make_async_copy(every, every, recv_sem).wait()
    pltpu.make_async_copy(every, every, send_sem).wait()


def solve_kernel(points, width, live, profile, match, new_profile, wall_stress):
    step = 1.0 / (points - 1)
    inv_step = float(points - 1)
    tiles = points // SUB
    sub = lax.broadcasted_iota(jnp.int32, (SUB, LANE), 0)
    lane = lax.broadcasted_iota(jnp.int32, (1, LANE), 1)
    index = [(sub + t * SUB).astype(jnp.float32) for t in range(tiles)]
    mixing = [0.41 * (i + 0.5) * step for i in index]
    mix_sq = [m * m for m in mixing]
    first = pl.program_id(0) * width

    def spread(row):
        return jnp.broadcast_to(row, (SUB, LANE))

    for cb in range(width // LANE):
        cols = pl.ds(cb * LANE, LANE)
        m = [spread(match[cb, q : q + 1, :]) for q in range(5)]
        visc = 0.01 * jnp.exp(0.5 * m[4])
        sigma = (0.5 * step) * m[3]
        speed = jnp.sqrt(m[1] * m[1] + m[2] * m[2] + 0.25)
        old = [profile[pl.ds(t * SUB, SUB), cols] for t in range(tiles)]
        turned = [pltpu.roll(u, SUB - 1, 0) for u in old]
        grad = []
        for t in range(tiles):
            after = turned[t + 1] if t + 1 < tiles else old[t]
            grad.append((jnp.where(sub == SUB - 1, after, turned[t]) - old[t]) * inv_step)
        for sweep in range(ITERS):
            weight_sum = jnp.zeros((SUB, LANE), jnp.float32)
            known_sum = jnp.zeros((SUB, LANE), jnp.float32)
            weights = []
            knowns = []
            for t in range(tiles):
                square = grad[t] * grad[t]
                over = square + 1.0
                inv_root = lax.rsqrt(over)
                viscous = visc + mix_sq[t] * (over * inv_root)
                excess = mix_sq[t] * (square * inv_root)
                weight = 1.0 / (viscous + excess)
                if t == tiles - 1:
                    weight = jnp.where(sub == SUB - 1, 0.0, weight)
                known = (excess * grad[t] + sigma * index[t]) * weight
                weight_sum = weight_sum + weight
                known_sum = known_sum + known
                weights.append(weight)
                knowns.append(known)
            weight_all = spread(jnp.sum(weight_sum, axis=0, keepdims=True))
            known_all = spread(jnp.sum(known_sum, axis=0, keepdims=True))
            flux = (inv_step * speed - known_all) / weight_all
            grad = [knowns[t] + flux * weights[t] for t in range(tiles)]
        burning = lane + (first + cb * LANE) < live[0]
        burn = spread(burning.astype(jnp.int32)) > 0
        carry = jnp.zeros((SUB, LANE), jnp.float32)
        for t in range(tiles):
            total = grad[t]
            for hop in (1, 2, 4):
                total = total + jnp.where(sub >= hop, pltpu.roll(total, hop, 0), 0.0)
            before = jnp.where(sub >= 1, pltpu.roll(total, 1, 0), 0.0)
            new_profile[pl.ds(t * SUB, SUB), cols] = jnp.where(
                burn, (before + carry) * step, old[t]
            )
            carry = carry + spread(total[SUB - 1 : SUB, :])
        shear = jnp.exp(0.3 * m[0]) * visc * spread(grad[0][0:1, :])
        for row, part in enumerate((m[1], m[2])):
            wall_stress[row : row + 1, cols] = jnp.where(burn, shear * part / speed, 0.0)[0:1, :]


def solve(profile, match, live):
    points, owned = profile.shape
    width = min(1024, owned)
    return pl.pallas_call(
        functools.partial(solve_kernel, points, width),
        grid=(owned // width,),
        out_shape=(
            jax.ShapeDtypeStruct((points, owned), jnp.float32),
            jax.ShapeDtypeStruct((2, owned), jnp.float32),
        ),
        in_specs=[
            pl.BlockSpec(memory_space=pltpu.SMEM),
            pl.BlockSpec((points, width), lambda i: (0, i)),
            pl.BlockSpec((width // LANE, SUB, LANE), lambda i: (i, 0, 0)),
        ],
        out_specs=(
            pl.BlockSpec((points, width), lambda i: (0, i)),
            pl.BlockSpec((2, width), lambda i: (0, i)),
        ),
        compiler_params=pltpu.CompilerParams(vmem_limit_bytes=32 << 20),
        name="wall_solve",
    )(live, profile, match)


def body(state, profile, samp_cell, own_live):
    comps, slab, section = state.shape
    owned = profile.shape[1]
    devices = lax.axis_size(AXES)
    slots = samp_cell.shape[2]
    here = lax.axis_index(AXES)
    groups = owned // LANE
    tiles_x = slab // SUB
    sections = section // LANE
    plane = slab * sections
    stride = plane + SUB
    cells = samp_cell.reshape(groups, LANE)
    view = state.reshape(comps, tiles_x, SUB, sections, LANE).transpose(0, 1, 3, 2, 4)
    arrived = pl.pallas_call(
        functools.partial(sample_kernel, AXES, (tiles_x, sections, stride)),
        out_shape=jax.ShapeDtypeStruct((devices, SUB, LANE), jnp.float32),
        in_specs=[
            pl.BlockSpec(memory_space=pltpu.VMEM),
            pl.BlockSpec(memory_space=pl.ANY),
        ],
        out_specs=pl.BlockSpec(memory_space=pltpu.VMEM),
        scratch_shapes=[
            pltpu.VMEM((comps, tiles_x, sections, SUB, LANE), jnp.float32),
            pltpu.VMEM((SUB * stride, LANE), jnp.float32),
            pltpu.VMEM((2, comps, sections, LANE), jnp.float32),
            pltpu.VMEM((groups, SUB, LANE), jnp.float32),
            pltpu.VMEM((groups, LANE), jnp.int32),
            pltpu.SMEM((groups, LANE), jnp.int32),
            pltpu.SemaphoreType.DMA((comps,)),
            pltpu.SemaphoreType.DMA((2, comps)),
            pltpu.SemaphoreType.DMA((2, comps)),
            pltpu.SemaphoreType.DMA,
            pltpu.SemaphoreType.DMA,
            pltpu.SemaphoreType.DMA,
        ],
        compiler_params=pltpu.CompilerParams(
            vmem_limit_bytes=60 << 20, collective_id=0, has_side_effects=True
        ),
        name="sample_cells",
    )(cells, view)
    if slots == LANE:
        match = arrived
    else:
        own = lax.dynamic_slice_in_dim(arrived, here % (LANE // slots) * slots, slots, axis=2)
        match = own.transpose(1, 0, 2).reshape(SUB, groups, LANE).transpose(1, 0, 2)
    live = lax.dynamic_slice(own_live, (here,), (1,))
    return solve(profile, match, live)


def solution(mesh):
    return jax.shard_map(
        body,
        mesh=mesh,
        in_specs=(
            P(None, "axial", "azim"),
            P(None, AXES),
            P(AXES, None, None),
            P(),
        ),
        out_specs=(P(None, AXES), P(None, AXES)),
        check_vma=False,
    )
```

```python
import functools

import jax
import jax.numpy as jnp
from jax import lax
from jax.experimental import pallas as pl
from jax.experimental.pallas import tpu as pltpu
from jax.sharding import PartitionSpec as P

ITERS = 3
AXES = ("axial", "azim")
SUB = 8
LANE = 128
WIDE = 256
PARTS = 4


def smooth_planes(raw, filt, stride, tiles_x, sections, sems, state):
    comps = state.shape[0]
    sub = lax.broadcasted_iota(jnp.int32, (SUB, LANE), 0)
    for q in range(comps):
        pltpu.make_async_copy(state.at[q], raw.at[q], sems.at[q]).wait()

        def section(tb, carry):
            tiles = [raw[q, xt, tb] for xt in range(tiles_x)]
            ups = [pltpu.roll(tile, 1, 0) for tile in tiles]
            downs = [pltpu.roll(tile, SUB - 1, 0) for tile in tiles]
            for xt in range(tiles_x):
                below = ups[xt - 1] if xt > 0 else 0.0
                above = downs[xt + 1] if xt + 1 < tiles_x else 0.0
                low = jnp.where(sub == 0, below, ups[xt])
                high = jnp.where(sub == SUB - 1, above, downs[xt])
                at = q * stride + (xt * sections + tb) * SUB
                filt[pl.ds(pl.multiple_of(at, SUB), SUB), :] = 0.25 * (low + high) + 0.5 * tiles[xt]
            return carry

        lax.fori_loop(0, sections, section, 0, unroll=8)


def add_halo(filt, halo, start, sections):
    for g in range(sections // SUB):
        rows = pl.ds(start + g * SUB * SUB, SUB, stride=SUB)
        filt[rows, :] = filt[rows, :] + 0.25 * halo[pl.ds(g * SUB, SUB), :]


def sample_kernel(
    names,
    sizes,
    cells,
    state,
    out,
    raw,
    filt,
    halo,
    stage,
    rows_v,
    rows,
    sems,
    halo_send,
    halo_recv,
    row_sem,
    send_sem,
    recv_sem,
):
    tiles_x, sections, stride = sizes
    comps = state.shape[0]
    groups = stage.shape[0]
    devices = out.shape[0]
    share = devices // groups
    axial, azim = names
    a, z = lax.axis_index(axial), lax.axis_index(azim)
    count, width = lax.axis_size(axial), lax.axis_size(azim)
    me = a * width + z

    def place(d):
        return (d // width, d % width)

    for q in range(comps):
        pltpu.make_async_copy(state.at[q], raw.at[q], sems.at[q]).start()

    barrier = pltpu.get_barrier_semaphore()

    def greet(j, carry):
        pl.semaphore_signal(
            barrier, inc=1, device_id=place((me + j) % devices), device_id_type=pl.DeviceIdType.MESH
        )
        return carry

    lax.fori_loop(1, devices, greet, 0)

    cell = cells[...]
    section = sections * LANE
    at_x = cell // section
    at_t = cell % section
    rows_v[...] = ((at_x // SUB) * sections + at_t // LANE) * SUB + at_x % SUB
    row_copy = pltpu.make_async_copy(rows_v, rows, row_sem)
    row_copy.start()
    pl.semaphore_wait(barrier, devices - 1)

    halos = []
    for q in range(comps):
        for side in range(2):
            if side == 0:
                edge = state.at[q, tiles_x - 1, :, SUB - 1, :]
                target = (a + 1) % count
            else:
                edge = state.at[q, 0, :, 0, :]
                target = (a + count - 1) % count
            copy = pltpu.make_async_remote_copy(
                src_ref=edge,
                dst_ref=halo.at[side, q],
                send_sem=halo_send.at[side, q],
                recv_sem=halo_recv.at[side, q],
                device_id=(target, z),
                device_id_type=pl.DeviceIdType.MESH,
            )
            copy.start()
            halos.append(copy)

    filt[pl.ds(comps * stride, (SUB - comps) * stride), :] = jnp.zeros(
        ((SUB - comps) * stride, LANE), jnp.float32
    )
    smooth_planes(raw, filt, stride, tiles_x, sections, sems, state)
    last = (tiles_x - 1) * sections * SUB + SUB - 1
    for q in range(comps):
        for side in range(2):
            halos[2 * q + side].wait()
            add_halo(filt, halo.at[side, q], q * stride + (0 if side == 0 else last), sections)
    row_copy.wait()
    lane = lax.broadcasted_iota(jnp.int32, (SUB, LANE), 1)

    def group(j, carry):
        g = (me // share + 1 + j) % groups
        wanted = jnp.broadcast_to(cells[pl.ds(g, 1), :] % LANE, (SUB, LANE))
        parts = [jnp.zeros((SUB, LANE), jnp.float32)] * PARTS
        for k in range(LANE):
            piece = filt[pl.ds(rows[g, k], SUB, stride=stride), :]
            piece = jnp.take_along_axis(piece, wanted, axis=1)
            parts[k % PARTS] = jnp.where(lane == k, piece, parts[k % PARTS])
        found = parts[0]
        for i in range(1, PARTS):
            found = jnp.where(lane % PARTS == i, parts[i], found)
        stage[g] = found
        for r in range(share):
            owner = g * share + r

            @pl.when(owner != me)
            def _():
                pltpu.make_async_remote_copy(
                    src_ref=stage.at[g],
                    dst_ref=out.at[me],
                    send_sem=send_sem,
                    recv_sem=recv_sem,
                    device_id=place(owner),
                    device_id_type=pl.DeviceIdType.MESH,
                ).start()

            @pl.when(owner == me)
            def _():
                out[me] = found

        return carry

    lax.fori_loop(0, groups, group, 0)
    every = out.at[pl.ds(0, devices - 1)]
    pltpu.make_async_copy(every, every, recv_sem).wait()
    pltpu.make_async_copy(every, every, send_sem).wait()


def solve_kernel(names, points, width, live, profile, match, new_profile, wall_stress):
    step = 1.0 / (points - 1)
    inv_step = float(points - 1)
    tiles = points // SUB
    sub = lax.broadcasted_iota(jnp.int32, (SUB, WIDE), 0)
    lane = lax.broadcasted_iota(jnp.int32, (1, WIDE), 1)
    index = [(sub + t * SUB).astype(jnp.float32) for t in range(tiles)]
    mixing = [0.41 * (i + 0.5) * step for i in index]
    mix_sq = [m * m for m in mixing]
    first = pl.program_id(0) * width
    live_here = live[lax.axis_index(names[0]) * lax.axis_size(names[1]) + lax.axis_index(names[1])]

    def spread(row):
        return jnp.broadcast_to(row, (SUB, WIDE))

    for cb in range(width // WIDE):
        cols = pl.ds(cb * WIDE, WIDE)
        tile = jnp.concatenate(
            [match[cb * (WIDE // LANE) + i] for i in range(WIDE // LANE)], axis=1
        )
        m = [spread(tile[q : q + 1, :]) for q in range(5)]
        visc = 0.01 * jnp.exp(0.5 * m[4])
        sigma = (0.5 * step) * m[3]
        speed = jnp.sqrt(m[1] * m[1] + m[2] * m[2] + 0.25)
        old = [profile[pl.ds(t * SUB, SUB), cols] for t in range(tiles)]
        turned = [pltpu.roll(u, SUB - 1, 0) for u in old]
        grad = []
        for t in range(tiles):
            after = turned[t + 1] if t + 1 < tiles else old[t]
            grad.append((jnp.where(sub == SUB - 1, after, turned[t]) - old[t]) * inv_step)
        for sweep in range(ITERS):
            weight_sum = jnp.zeros((SUB, WIDE), jnp.float32)
            known_sum = jnp.zeros((SUB, WIDE), jnp.float32)
            weights = []
            knowns = []
            for t in range(tiles):
                square = grad[t] * grad[t]
                over = square + 1.0
                inv_root = lax.rsqrt(over)
                viscous = visc + mix_sq[t] * (over * inv_root)
                excess = mix_sq[t] * (square * inv_root)
                weight = 1.0 / (viscous + excess)
                if t == tiles - 1:
                    weight = jnp.where(sub == SUB - 1, 0.0, weight)
                known = (excess * grad[t] + sigma * index[t]) * weight
                weight_sum = weight_sum + weight
                known_sum = known_sum + known
                weights.append(weight)
                knowns.append(known)
            weight_all = spread(jnp.sum(weight_sum, axis=0, keepdims=True))
            known_all = spread(jnp.sum(known_sum, axis=0, keepdims=True))
            flux = (inv_step * speed - known_all) / weight_all
            grad = [knowns[t] + flux * weights[t] for t in range(tiles)]
        burning = lane + (first + cb * WIDE) < live_here
        burn = spread(burning.astype(jnp.int32)) > 0
        carry = jnp.zeros((SUB, WIDE), jnp.float32)
        for t in range(tiles):
            total = grad[t]
            for hop in (1, 2, 4):
                total = total + jnp.where(sub >= hop, pltpu.roll(total, hop, 0), 0.0)
            before = jnp.where(sub >= 1, pltpu.roll(total, 1, 0), 0.0)
            new_profile[pl.ds(t * SUB, SUB), cols] = jnp.where(
                burn, (before + carry) * step, old[t]
            )
            carry = carry + spread(total[SUB - 1 : SUB, :])
        shear = jnp.exp(0.3 * m[0]) * visc * spread(grad[0][0:1, :])
        for row, part in enumerate((m[1], m[2])):
            wall_stress[row : row + 1, cols] = jnp.where(burn, shear * part / speed, 0.0)[0:1, :]


def solve(profile, match, live):
    points, owned = profile.shape
    width = min(1024, owned)
    return pl.pallas_call(
        functools.partial(solve_kernel, AXES, points, width),
        grid=(owned // width,),
        out_shape=(
            jax.ShapeDtypeStruct((points, owned), jnp.float32),
            jax.ShapeDtypeStruct((2, owned), jnp.float32),
        ),
        in_specs=[
            pl.BlockSpec(memory_space=pltpu.SMEM),
            pl.BlockSpec((points, width), lambda i: (0, i)),
            pl.BlockSpec((width // LANE, SUB, LANE), lambda i: (i, 0, 0)),
        ],
        out_specs=(
            pl.BlockSpec((points, width), lambda i: (0, i)),
            pl.BlockSpec((2, width), lambda i: (0, i)),
        ),
        compiler_params=pltpu.CompilerParams(vmem_limit_bytes=60 << 20),
        name="wall_solve",
    )(live, profile, match)


def body(state, profile, samp_cell, own_live):
    comps, slab, section = state.shape
    owned = profile.shape[1]
    devices = lax.axis_size(AXES)
    slots = samp_cell.shape[2]
    here = lax.axis_index(AXES)
    groups = owned // LANE
    tiles_x = slab // SUB
    sections = section // LANE
    plane = slab * sections
    stride = plane + SUB
    cells = samp_cell.reshape(groups, LANE)
    view = state.reshape(comps, tiles_x, SUB, sections, LANE).transpose(0, 1, 3, 2, 4)
    arrived = pl.pallas_call(
        functools.partial(sample_kernel, AXES, (tiles_x, sections, stride)),
        out_shape=jax.ShapeDtypeStruct((devices, SUB, LANE), jnp.float32),
        in_specs=[
            pl.BlockSpec(memory_space=pltpu.VMEM),
            pl.BlockSpec(memory_space=pl.ANY),
        ],
        out_specs=pl.BlockSpec(memory_space=pltpu.VMEM),
        scratch_shapes=[
            pltpu.VMEM((comps, tiles_x, sections, SUB, LANE), jnp.float32),
            pltpu.VMEM((SUB * stride, LANE), jnp.float32),
            pltpu.VMEM((2, comps, sections, LANE), jnp.float32),
            pltpu.VMEM((groups, SUB, LANE), jnp.float32),
            pltpu.VMEM((groups, LANE), jnp.int32),
            pltpu.SMEM((groups, LANE), jnp.int32),
            pltpu.SemaphoreType.DMA((comps,)),
            pltpu.SemaphoreType.DMA((2, comps)),
            pltpu.SemaphoreType.DMA((2, comps)),
            pltpu.SemaphoreType.DMA,
            pltpu.SemaphoreType.DMA,
            pltpu.SemaphoreType.DMA,
        ],
        compiler_params=pltpu.CompilerParams(
            vmem_limit_bytes=60 << 20, collective_id=0, has_side_effects=True
        ),
        name="sample_cells",
    )(cells, view)
    if slots == LANE:
        match = arrived
    else:
        own = lax.dynamic_slice_in_dim(arrived, here % (LANE // slots) * slots, slots, axis=2)
        match = own.transpose(1, 0, 2).reshape(SUB, groups, LANE).transpose(1, 0, 2)
    return solve(profile, match, own_live)


def solution(mesh):
    return jax.shard_map(
        body,
        mesh=mesh,
        in_specs=(
            P(None, "axial", "azim"),
            P(None, AXES),
            P(AXES, None, None),
            P(),
        ),
        out_specs=(P(None, AXES), P(None, AXES)),
        check_vma=False,
    )
```

```python
import functools

import jax
import jax.numpy as jnp
from jax import lax
from jax.experimental import pallas as pl
from jax.experimental.pallas import tpu as pltpu
from jax.sharding import PartitionSpec as P

ITERS = 3
AXES = ("axial", "azim")
SUB = 8
LANE = 128
WIDE = 256
PARTS = 4


def smooth_planes(raw, filt, stride, tiles_x, sections, sems, state):
    comps = state.shape[0]
    sub = lax.broadcasted_iota(jnp.int32, (SUB, LANE), 0)
    for q in range(comps):
        pltpu.make_async_copy(state.at[q], raw.at[q], sems.at[q]).wait()

        def section(tb, carry):
            tiles = [raw[q, xt, tb] for xt in range(tiles_x)]
            ups = [pltpu.roll(tile, 1, 0) for tile in tiles]
            downs = [pltpu.roll(tile, SUB - 1, 0) for tile in tiles]
            for xt in range(tiles_x):
                below = ups[xt - 1] if xt > 0 else 0.0
                above = downs[xt + 1] if xt + 1 < tiles_x else 0.0
                low = jnp.where(sub == 0, below, ups[xt])
                high = jnp.where(sub == SUB - 1, above, downs[xt])
                at = q * stride + (xt * sections + tb) * SUB
                filt[pl.ds(pl.multiple_of(at, SUB), SUB), :] = 0.25 * (low + high) + 0.5 * tiles[xt]
            return carry

        lax.fori_loop(0, sections, section, 0, unroll=8)


def add_halo(filt, halo, start, sections):
    for g in range(sections // SUB):
        rows = pl.ds(start + g * SUB * SUB, SUB, stride=SUB)
        filt[rows, :] = filt[rows, :] + 0.25 * halo[pl.ds(g * SUB, SUB), :]


def sample_kernel(
    names,
    sizes,
    cells,
    state,
    out,
    raw,
    filt,
    halo,
    stage,
    rows_v,
    rows,
    sems,
    halo_send,
    halo_recv,
    row_sem,
    send_sem,
    recv_sem,
):
    tiles_x, sections, stride = sizes
    comps = state.shape[0]
    groups = stage.shape[0]
    devices = out.shape[0]
    share = devices // groups
    axial, azim = names
    a, z = lax.axis_index(axial), lax.axis_index(azim)
    count, width = lax.axis_size(axial), lax.axis_size(azim)
    me = a * width + z

    def place(d):
        return (d // width, d % width)

    for q in range(comps):
        pltpu.make_async_copy(state.at[q], raw.at[q], sems.at[q]).start()

    barrier = pltpu.get_barrier_semaphore()

    def greet(j, carry):
        pl.semaphore_signal(
            barrier, inc=1, device_id=place((me + j) % devices), device_id_type=pl.DeviceIdType.MESH
        )
        return carry

    lax.fori_loop(1, devices, greet, 0)

    cell = cells[...]
    section = sections * LANE
    at_x = cell // section
    at_t = cell % section
    rows_v[...] = ((at_x // SUB) * sections + at_t // LANE) * SUB + at_x % SUB
    row_copy = pltpu.make_async_copy(rows_v, rows, row_sem)
    row_copy.start()
    pl.semaphore_wait(barrier, devices - 1)

    halos = []
    for q in range(comps):
        for side in range(2):
            if side == 0:
                edge = state.at[q, tiles_x - 1, :, SUB - 1, :]
                target = (a + 1) % count
            else:
                edge = state.at[q, 0, :, 0, :]
                target = (a + count - 1) % count
            copy = pltpu.make_async_remote_copy(
                src_ref=edge,
                dst_ref=halo.at[side, q],
                send_sem=halo_send.at[side, q],
                recv_sem=halo_recv.at[side, q],
                device_id=(target, z),
                device_id_type=pl.DeviceIdType.MESH,
            )
            copy.start()
            halos.append(copy)

    filt[pl.ds(comps * stride, (SUB - comps) * stride), :] = jnp.zeros(
        ((SUB - comps) * stride, LANE), jnp.float32
    )
    smooth_planes(raw, filt, stride, tiles_x, sections, sems, state)
    last = (tiles_x - 1) * sections * SUB + SUB - 1
    for q in range(comps):
        for side in range(2):
            halos[2 * q + side].wait()
            add_halo(filt, halo.at[side, q], q * stride + (0 if side == 0 else last), sections)
    row_copy.wait()
    lane = lax.broadcasted_iota(jnp.int32, (SUB, LANE), 1)

    def group(j, carry):
        g = (me // share + 1 + j) % groups
        wanted = jnp.broadcast_to(cells[pl.ds(g, 1), :] % LANE, (SUB, LANE))
        parts = [jnp.zeros((SUB, LANE), jnp.float32)] * PARTS
        for k in range(LANE):
            piece = filt[pl.ds(rows[g, k], SUB, stride=stride), :]
            piece = jnp.take_along_axis(piece, wanted, axis=1)
            parts[k % PARTS] = jnp.where(lane == k, piece, parts[k % PARTS])
        found = parts[0]
        for i in range(1, PARTS):
            found = jnp.where(lane % PARTS == i, parts[i], found)
        stage[g] = found
        for r in range(share):
            owner = g * share + r

            @pl.when(owner != me)
            def _():
                pltpu.make_async_remote_copy(
                    src_ref=stage.at[g],
                    dst_ref=out.at[me],
                    send_sem=send_sem,
                    recv_sem=recv_sem,
                    device_id=place(owner),
                    device_id_type=pl.DeviceIdType.MESH,
                ).start()

            @pl.when(owner == me)
            def _():
                out[me] = found

        return carry

    lax.fori_loop(0, groups, group, 0)
    every = out.at[pl.ds(0, devices - 1)]
    pltpu.make_async_copy(every, every, recv_sem).wait()
    pltpu.make_async_copy(every, every, send_sem).wait()


def solve_kernel(
    names, points, width, live, stored, match, solved, wall_stress, profile, new_profile, sems_in, sems_out
):
    chunks = [pl.ds(c * width, width) for c in range(profile.shape[1] // width)]
    arrivals = []
    for c, part in enumerate(chunks):
        arrivals.append(pltpu.make_async_copy(stored.at[:, part], profile.at[:, part], sems_in.at[c]))
        arrivals[c].start()
    departures = []
    step = 1.0 / (points - 1)
    inv_step = float(points - 1)
    tiles = points // SUB
    sub = lax.broadcasted_iota(jnp.int32, (SUB, WIDE), 0)
    lane = lax.broadcasted_iota(jnp.int32, (1, WIDE), 1)
    index = [(sub + t * SUB).astype(jnp.float32) for t in range(tiles)]
    mixing = [0.41 * (i + 0.5) * step for i in index]
    mix_sq = [m * m for m in mixing]
    live_here = live[lax.axis_index(names[0]) * lax.axis_size(names[1]) + lax.axis_index(names[1])]

    def spread(row):
        return jnp.broadcast_to(row, (SUB, WIDE))

    for cb in range(profile.shape[1] // WIDE):
        if cb * WIDE % width == 0:
            arrivals[cb * WIDE // width].wait()
        cols = pl.ds(cb * WIDE, WIDE)
        tile = jnp.concatenate(
            [match[cb * (WIDE // LANE) + i] for i in range(WIDE // LANE)], axis=1
        )
        m = [spread(tile[q : q + 1, :]) for q in range(5)]
        visc = 0.01 * jnp.exp(0.5 * m[4])
        sigma = (0.5 * step) * m[3]
        speed = jnp.sqrt(m[1] * m[1] + m[2] * m[2] + 0.25)
        old = [profile[pl.ds(t * SUB, SUB), cols] for t in range(tiles)]
        turned = [pltpu.roll(u, SUB - 1, 0) for u in old]
        grad = []
        for t in range(tiles):
            after = turned[t + 1] if t + 1 < tiles else old[t]
            grad.append((jnp.where(sub == SUB - 1, after, turned[t]) - old[t]) * inv_step)
        for sweep in range(ITERS):
            weight_sum = jnp.zeros((SUB, WIDE), jnp.float32)
            known_sum = jnp.zeros((SUB, WIDE), jnp.float32)
            weights = []
            knowns = []
            for t in range(tiles):
                square = grad[t] * grad[t]
                over = square + 1.0
                inv_root = lax.rsqrt(over)
                viscous = visc + mix_sq[t] * (over * inv_root)
                excess = mix_sq[t] * (square * inv_root)
                weight = 1.0 / (viscous + excess)
                if t == tiles - 1:
                    weight = jnp.where(sub == SUB - 1, 0.0, weight)
                known = (excess * grad[t] + sigma * index[t]) * weight
                weight_sum = weight_sum + weight
                known_sum = known_sum + known
                weights.append(weight)
                knowns.append(known)
            weight_all = spread(jnp.sum(weight_sum, axis=0, keepdims=True))
            known_all = spread(jnp.sum(known_sum, axis=0, keepdims=True))
            flux = (inv_step * speed - known_all) / weight_all
            grad = [knowns[t] + flux * weights[t] for t in range(tiles)]
        burning = lane + cb * WIDE < live_here
        burn = spread(burning.astype(jnp.int32)) > 0
        carry = jnp.zeros((SUB, WIDE), jnp.float32)
        for t in range(tiles):
            total = grad[t]
            for hop in (1, 2, 4):
                total = total + jnp.where(sub >= hop, pltpu.roll(total, hop, 0), 0.0)
            before = jnp.where(sub >= 1, pltpu.roll(total, 1, 0), 0.0)
            new_profile[pl.ds(t * SUB, SUB), cols] = jnp.where(
                burn, (before + carry) * step, old[t]
            )
            carry = carry + spread(total[SUB - 1 : SUB, :])
        shear = jnp.exp(0.3 * m[0]) * visc * spread(grad[0][0:1, :])
        for row, part in enumerate((m[1], m[2])):
            wall_stress[row : row + 1, cols] = jnp.where(burn, shear * part / speed, 0.0)[0:1, :]
        if (cb + 1) * WIDE % width == 0:
            c = cb * WIDE // width
            part = chunks[c]
            departures.append(
                pltpu.make_async_copy(new_profile.at[:, part], solved.at[:, part], sems_out.at[c])
            )
            departures[c].start()
    for departure in departures:
        departure.wait()


def solve(profile, match, live):
    points, owned = profile.shape
    width = min(512, owned)
    return pl.pallas_call(
        functools.partial(solve_kernel, AXES, points, width),
        out_shape=(
            jax.ShapeDtypeStruct((points, owned), jnp.float32),
            jax.ShapeDtypeStruct((2, owned), jnp.float32),
        ),
        in_specs=[
            pl.BlockSpec(memory_space=pltpu.SMEM),
            pl.BlockSpec(memory_space=pl.ANY),
            pl.BlockSpec(memory_space=pltpu.VMEM),
        ],
        out_specs=(
            pl.BlockSpec(memory_space=pl.ANY),
            pl.BlockSpec(memory_space=pltpu.VMEM),
        ),
        scratch_shapes=[
            pltpu.VMEM((points, owned), jnp.float32),
            pltpu.VMEM((points, owned), jnp.float32),
            pltpu.SemaphoreType.DMA((owned // width,)),
            pltpu.SemaphoreType.DMA((owned // width,)),
        ],
        compiler_params=pltpu.CompilerParams(vmem_limit_bytes=60 << 20),
        name="wall_solve",
    )(live, profile, match)


def body(state, profile, samp_cell, own_live):
    comps, slab, section = state.shape
    owned = profile.shape[1]
    devices = lax.axis_size(AXES)
    slots = samp_cell.shape[2]
    here = lax.axis_index(AXES)
    groups = owned // LANE
    tiles_x = slab // SUB
    sections = section // LANE
    plane = slab * sections
    stride = plane + SUB
    cells = samp_cell.reshape(groups, LANE)
    view = state.reshape(comps, tiles_x, SUB, sections, LANE).transpose(0, 1, 3, 2, 4)
    arrived = pl.pallas_call(
        functools.partial(sample_kernel, AXES, (tiles_x, sections, stride)),
        out_shape=jax.ShapeDtypeStruct((devices, SUB, LANE), jnp.float32),
        in_specs=[
            pl.BlockSpec(memory_space=pltpu.VMEM),
            pl.BlockSpec(memory_space=pl.ANY),
        ],
        out_specs=pl.BlockSpec(memory_space=pltpu.VMEM),
        scratch_shapes=[
            pltpu.VMEM((comps, tiles_x, sections, SUB, LANE), jnp.float32),
            pltpu.VMEM((SUB * stride, LANE), jnp.float32),
            pltpu.VMEM((2, comps, sections, LANE), jnp.float32),
            pltpu.VMEM((groups, SUB, LANE), jnp.float32),
            pltpu.VMEM((groups, LANE), jnp.int32),
            pltpu.SMEM((groups, LANE), jnp.int32),
            pltpu.SemaphoreType.DMA((comps,)),
            pltpu.SemaphoreType.DMA((2, comps)),
            pltpu.SemaphoreType.DMA((2, comps)),
            pltpu.SemaphoreType.DMA,
            pltpu.SemaphoreType.DMA,
            pltpu.SemaphoreType.DMA,
        ],
        compiler_params=pltpu.CompilerParams(
            vmem_limit_bytes=60 << 20, collective_id=0, has_side_effects=True
        ),
        name="sample_cells",
    )(cells, view)
    if slots == LANE:
        match = arrived
    else:
        own = lax.dynamic_slice_in_dim(arrived, here % (LANE // slots) * slots, slots, axis=2)
        match = own.transpose(1, 0, 2).reshape(SUB, groups, LANE).transpose(1, 0, 2)
    return solve(profile, match, own_live)


def solution(mesh):
    return jax.shard_map(
        body,
        mesh=mesh,
        in_specs=(
            P(None, "axial", "azim"),
            P(None, AXES),
            P(AXES, None, None),
            P(),
        ),
        out_specs=(P(None, AXES), P(None, AXES)),
        check_vma=False,
    )
```
